32 devices in a mesh: dp: 8 (over y, x, core), tensor: 4 (over z).
Axes of the slice: x: 2, y: 2, z: 4, core: 2. Of those that a mesh axis runs over, the one named last changes fastest.
Arguments:
- activations: bfloat16 [160, 6656], P('dp', 'tensor'), may hold values from -6 to 6
- weight_codes: int32 [6656, 8192], P(('tensor', 'dp')), may hold values from 0 to 15
- scale_index: int32 [6656, 64], P(('tensor', 'dp')), may hold values from 0 to 15, as said below
- scale_table: float32 [16], replicated
- bit_widths: int32 [1, 6656, 64], P(None, ('tensor', 'dp')), may hold values from 2 to 4
Outputs:
- base_output: bfloat16 [160, 8192], P('tensor', 'dp')
- scores: float32 [1, 160], P(None, 'tensor')
The draws below stay inside these ranges and needn't reach their ends.
Inputs may be any that keep to these rules, and one draw needn't show every extreme that they name: `scale_index`: an entry of scale_table for each row and each group of 128 columns.
All inputs are finite; a program needn't handle non-finite values.
Results may differ from the reference program's by a relative error of at most 0.0058.
Values may be sent and summed in bfloat16 or wider, within the bound.
A program may use at most 128 MiB of HBM per device.

```python
import math
import jax
import jax.numpy as jnp
from jax import lax

D = 8192
FF_DEV = 1664
HB = 128
GROUP = 128
NSCALE = 16
NCAND = 1
FFW = 6656
TOKENS = 160
NGRP = 64
N_TENSOR = 4


def draw_scale_index(key, part):
    noise = jax.random.randint(key, (FFW, NGRP), 0, 4)
    level = (NSCALE - 3) * jnp.arange(NGRP, dtype=jnp.int32) // NGRP
    chosen = (noise + level[None, :]).astype(jnp.int32)
    chosen = chosen.at[0, 0].set(0)
    chosen = chosen.at[FFW - 1, NGRP - 1].set(NSCALE - 1)
    return chosen


def draw_scale_table(key, part):
    ladder = jnp.arange(NSCALE, dtype=jnp.float32) / (NSCALE - 1)
    factor = jax.random.uniform(key, (NSCALE,), jnp.float32, 0.8, 1.25)
    return 0.25 * FFW ** (-0.5) * jnp.exp(ladder * jnp.log(3.0)) * factor


def place_ends(entries, rng, smallest, largest):
    longest = entries.shape.index(max(entries.shape))
    spots = []
    for shift in (0, 1):
        where = [jax.random.randint(jax.random.fold_in(rng, axis), (), 0, length) for axis, length in enumerate(entries.shape)]
        where[longest] = (where[longest] + shift) % entries.shape[longest]
        spots.append(tuple(where))
    return entries.at[spots[0]].set(smallest).at[spots[1]].set(largest)


def level_of(key, dims, shards, low, largest):
    def one(axis_at, shards_of):
        draws = jax.random.uniform(jax.random.fold_in(jax.random.fold_in(key, 6), axis_at), (shards_of,), jnp.float32, low / len(shards), largest / len(shards))
        return jnp.repeat(jnp.exp(draws), dims[axis_at] // shards_of).reshape((-1,) + (1,) * (len(dims) - axis_at - 1))

    gain = one(*shards[0])
    for cut in shards[1:]:
        gain = gain * one(*cut)
    return gain


def gaussian(rng, extent, deviation, bound, pieces=(), held_as=jnp.bfloat16):
    result = deviation * jax.random.normal(rng, extent, jnp.float32)
    if pieces:
        result = result * level_of(rng, extent, pieces, -0.22, 0.18)
    return jnp.clip(result, -bound, bound).astype(held_as)


def setup_inputs(seed: int = 0) -> dict:
    seeds = jax.random.split(jax.random.key(seed), 6)
    return {
        "activations": gaussian(seeds[0], (TOKENS, FFW), 1.0, 6.0, ((0, 8), (1, 4))),
        "weight_codes": place_ends(jax.random.randint(seeds[1], (FFW, D), 0, 16), jax.random.fold_in(seeds[1], 1), 0, 15).astype(jnp.int32),
        "scale_index": draw_scale_index(jax.random.fold_in(seeds[5], 71), 0),
        "scale_table": draw_scale_table(jax.random.fold_in(seeds[5], 71), 0),
        "bit_widths": place_ends(jax.random.randint(seeds[4], (NCAND, FFW, NGRP), 2, 5), jax.random.fold_in(seeds[4], 1), 2, 4).astype(jnp.int32),
    }


score_divisor = 512.0

def sylvester(order_size):
    positions = jnp.arange(order_size, dtype=jnp.int32)
    intersection = positions[:, None] & positions[None, :]
    parity = jnp.zeros((order_size, order_size), jnp.int32)
    for shift_bit in range(max(order_size.bit_length() - 1, 0)):
        parity = parity + (intersection >> shift_bit & 1)
    parity = parity % 2
    return (1 - 2 * parity).astype(jnp.float32)

def rotate(activations):
    token_count = activations.shape[0]
    shaped = activations.astype(jnp.float32).reshape(token_count, N_TENSOR, FF_DEV // HB, HB)
    inner = jnp.einsum('tsnb,bc->tsnc', shaped, sylvester(HB), precision=lax.Precision.HIGHEST)
    outer = jnp.einsum('tsnc,js->tjnc', inner, sylvester(N_TENSOR), precision=lax.Precision.HIGHEST)
    scaled = outer * (1.0 / math.sqrt(HB * N_TENSOR))
    return scaled.reshape(token_count, FFW).astype(jnp.bfloat16)

def reference(activations, weight_codes, scale_index, scale_table, bit_widths):
    rotated = rotate(activations)

    def column_block(group_id):
        code_block = lax.dynamic_slice_in_dim(weight_codes, group_id * GROUP, GROUP, 1)
        index_block = lax.dynamic_slice_in_dim(scale_index, group_id, 1, 1)
        scale_block = scale_table[index_block]
        bits_block = lax.dynamic_slice_in_dim(bit_widths, group_id, 1, 2)
        base_weight = ((code_block - 8).astype(jnp.float32) * scale_block).astype(jnp.bfloat16)
        base_out = jnp.dot(rotated, base_weight, preferred_element_type=jnp.float32)
        step_size = jnp.where(bits_block == 2, 4, jnp.where(bits_block == 3, 2, 1)).astype(jnp.int32)
        cand_codes = code_block[None] // step_size * step_size + step_size // 2
        cand_weight = ((cand_codes - 8).astype(jnp.float32) * scale_block[None]).astype(jnp.bfloat16)
        errors = []
        for candidate in range(NCAND):
            cand_out = jnp.dot(rotated, cand_weight[candidate], preferred_element_type=jnp.float32)
            gap = cand_out - base_out
            errors.append(lax.optimization_barrier(jnp.sum(gap * gap, axis=1)) / score_divisor)
        return (base_out, jnp.stack(errors, 0))
    base_blocks, group_scores = lax.map(column_block, jnp.arange(NGRP, dtype=jnp.int32))
    base_output = jnp.transpose(base_blocks, (1, 0, 2)).reshape(TOKENS, D).astype(jnp.bfloat16)
    scores = lax.optimization_barrier(jnp.sum(group_scores, axis=0))
    return (base_output, scores)
```

```python
import functools
import math

import jax
import jax.numpy as jnp
import numpy as np
from jax import lax
from jax.experimental import pallas as pl
from jax.experimental.pallas import tpu as pltpu
from jax.sharding import PartitionSpec as P

HB = 128
SCORE_DIVISOR = 512.0
MESH = pl.DeviceIdType.MESH
BF16, F32, I32 = jnp.bfloat16, jnp.float32, jnp.int32


def sylvester(order):
    bits = np.arange(order)[:, None] & np.arange(order)[None, :]
    parity = np.zeros((order, order), np.int32)
    for shift in range(order.bit_length()):
        parity += (bits >> shift) & 1
    return (1 - 2 * (parity % 2)).astype(np.float32)


def up16(count):
    return -(-count // 16) * 16


def sizes(ndp, nt, act_shape, code_shape):
    tl, width = act_shape
    rows, model = code_shape
    z = dict(ndp=ndp, nt=nt, chips=ndp // 2, tl=tl, tp=up16(tl), nblk=width // HB, rows=rows)
    z["rp"] = up16(rows)
    z["cols"] = model // ndp
    z["tokens"] = tl * ndp
    z["tt"] = z["tokens"] // nt
    pair = 2 * rows
    spans = [(c * pair + pair - 1) // HB - c * pair // HB + 1 for c in range(z["chips"])]
    z["nb"] = min(max(spans), z["nblk"])
    z["cw"] = 256 if z["cols"] % 256 == 0 else z["cols"]
    z["nch"] = z["cols"] // z["cw"]
    return z


def window_start(z, chip):
    return jnp.minimum(chip * (2 * z["rows"]) // HB, z["nblk"] - z["nb"])


def kernel(z, act_ref, code_hbm, index_ref, table_ref, bits_ref, had_ref, out_ref, score_ref,
           codes, xs, rot, win, wpad, lhs, weights, wrecv, psend, prec, acc, zsend, zrec, srec,
           code_sem, xs_s, xs_r, win_s, win_r, w_s, w_r, p_s, p_r, z_s, z_r, s_s, s_r):
    ndp, nt, chips = z["ndp"], z["nt"], z["chips"]
    tl, tp, nblk, nb = z["tl"], z["tp"], z["nblk"], z["nb"]
    rows, rp, cols, tokens, tt = z["rows"], z["rp"], z["cols"], z["tokens"], z["tt"]
    cw, nch = z["cw"], z["nch"]
    d = lax.axis_index("dp")
    s = lax.axis_index("tensor")
    chip, core = d // 2, d % 2

    loads = []
    for q in range(chips):
        span = pl.ds(q * 2 * cols, 2 * cols)
        load = pltpu.make_async_copy(code_hbm.at[:, span], codes.at[:, span], code_sem.at[q])
        load.start()
        loads.append(load)

    barrier = pltpu.get_barrier_semaphore()
    for k in range(1, ndp):
        pl.semaphore_signal(barrier, inc=1, device_id=(lax.rem(d + k, ndp), s), device_id_type=MESH)
    for k in range(1, nt):
        pl.semaphore_signal(barrier, inc=1, device_id=(d, lax.rem(s + k, nt)), device_id_type=MESH)

    xs[0] = jnp.zeros(xs.shape[1:], BF16)
    for n in range(nblk):
        xs[0, n * tp:n * tp + tl, :] = act_ref[:, n * HB:(n + 1) * HB]

    pl.semaphore_wait(barrier, ndp - 1 + nt - 1)

    xcopies = []
    for k in range(1, nt):
        copy = pltpu.make_async_remote_copy(
            src_ref=xs.at[0], dst_ref=xs.at[k], send_sem=xs_s.at[k], recv_sem=xs_r.at[k],
            device_id=(d, lax.rem(s + k, nt)), device_id_type=MESH)
        copy.start()
        xcopies.append(copy)

    index = index_ref[...]
    scales = jnp.zeros(index.shape, F32)
    for i in range(table_ref.shape[0]):
        scales = jnp.where(index == i, table_ref[i], scales)
    bits = bits_ref[...]
    step = jnp.where(bits == 2, 4, jnp.where(bits == 3, 2, 1)).astype(I32)

    if rp != rows:
        weights[...] = jnp.zeros(weights.shape, BF16)
    groups = cols // HB
    wcopies = []

    def dequantize(q):
        rel = lax.rem(q - chip + chips, chips)
        loads[q].wait()
        for half in range(2):
            away = lax.rem(core + half, 2)
            for g in range(groups):
                gg = (q * 2 + half) * groups + g
                c = codes[:, gg * HB:(gg + 1) * HB]
                sc = scales[:, gg:gg + 1]
                st = step[:, gg:gg + 1]
                base = ((c - 8).astype(F32) * sc).astype(BF16)
                cand = (((c & -st) + ((st >> 1) - 8)).astype(F32) * sc).astype(BF16)
                gap = (cand.astype(F32) - base.astype(F32)).astype(BF16)
                weights[away, rel, 0, 0:rows, g * HB:(g + 1) * HB] = base
                weights[away, rel, 1, 0:rows, g * HB:(g + 1) * HB] = gap
        copy = pltpu.make_async_remote_copy(
            src_ref=weights.at[1, rel], dst_ref=wrecv.at[rel], send_sem=w_s.at[q],
            recv_sem=w_r.at[q], device_id=(chip * 2 + 1 - core, s), device_id_type=MESH)
        copy.start()
        wcopies.append(copy)

    def rotate():
        total = jnp.zeros((nblk * tp, HB), F32)
        for k in range(nt):
            if k:
                xcopies[k - 1].wait_recv()
            src = lax.rem(s - k + nt, nt)
            parity = 0
            for b in range(max(nt.bit_length() - 1, 0)):
                parity = parity + (src // 2 ** b % 2) * (s // 2 ** b % 2)
            sign = (1 - 2 * (parity % 2)).astype(F32)
            total = total + sign * jnp.dot(xs[k], had_ref[...], preferred_element_type=F32)
        rot[...] = (total * (1.0 / math.sqrt(HB * nt))).astype(BF16)
        copies = []
        for k in range(1, ndp):
            to = lax.rem(d + k, ndp)
            first = pl.multiple_of(window_start(z, to // 2) * tp, 16)
            copy = pltpu.make_async_remote_copy(
                src_ref=rot.at[pl.ds(first, nb * tp)], dst_ref=win.at[k], send_sem=win_s.at[k],
                recv_sem=win_r.at[k], device_id=(to, s), device_id_type=MESH)
            copy.start()
            copies.append(copy)
        return copies

    split = max(chips // 2, 1)
    for q in range(split):
        dequantize(q)
    wincopies = rotate()
    for q in range(split, chips):
        dequantize(q)

    mine = window_start(z, chip)
    first = pl.multiple_of(mine * tp, 16)
    win[0] = rot[pl.ds(first, nb * tp), :]
    for k in range(ndp):
        if k:
            wincopies[k - 1].wait_recv()
        for n in range(nb):
            wpad[k * tp:(k + 1) * tp, n * HB:(n + 1) * HB] = win[k, n * tp:(n + 1) * tp, :]
    t_id = lax.broadcasted_iota(I32, (tokens, ndp * tp), 0)
    q_id = lax.broadcasted_iota(I32, (tokens, ndp * tp), 1)
    slot = q_id // tp
    inner = q_id - slot * tp
    src = d - slot
    src = jnp.where(src < 0, src + ndp, src)
    pick = ((t_id == src * tl + inner) & (inner < tl)).astype(F32).astype(BF16)
    ordered = jnp.dot(pick, wpad[...], preferred_element_type=F32).astype(BF16)
    offset = chip * (2 * rows) - mine * HB
    f_id = lax.broadcasted_iota(I32, (nb * HB, rp), 0)
    r_id = lax.broadcasted_iota(I32, (nb * HB, rp), 1)
    for half in range(2):
        owner = lax.rem(core + half, 2)
        shift = ((f_id == offset + owner * rows + r_id) & (r_id < rows)).astype(F32).astype(BF16)
        lhs[half] = jnp.dot(ordered, shift, preferred_element_type=F32).astype(BF16)

    for copy in wcopies:
        copy.wait_recv()

    def product(k, kind, ch):
        span = slice(ch * cw, (ch + 1) * cw)
        return (jnp.dot(lhs[0], weights[0, k, kind, :, span], preferred_element_type=F32)
                + jnp.dot(lhs[1], wrecv[k, kind, :, span], preferred_element_type=F32))

    pcopies = {}
    for ch in range(nch):
        for k in range(1, chips):
            for kind in range(2):
                psend[k - 1, ch, kind] = product(k, kind, ch).astype(BF16)
            copy = pltpu.make_async_remote_copy(
                src_ref=psend.at[k - 1, ch], dst_ref=prec.at[k - 1, ch],
                send_sem=p_s.at[k - 1, ch], recv_sem=p_r.at[k - 1, ch],
                device_id=(lax.rem(chip + k, chips) * 2 + core, s), device_id_type=MESH)
            copy.start()
            pcopies[k, ch] = copy
        for kind in range(2):
            acc[ch, kind] = product(0, kind, ch)

    zcopies = {}
    for ch in range(nch):
        for k in range(1, chips):
            pcopies[k, ch].wait_recv()
        for kind in range(2):
            total = acc[ch, kind]
            for k in range(1, chips):
                total = total + prec[k - 1, ch, kind].astype(F32)
            acc[ch, kind] = total
        for k in range(1, nt):
            to = lax.rem(s + k, nt)
            part = pl.ds(pl.multiple_of(to * tt, 8), tt)
            zsend[k - 1, ch] = jnp.concatenate(
                [acc[ch, 0, part, :], acc[ch, 1, part, :]], axis=0).astype(BF16)
            copy = pltpu.make_async_remote_copy(
                src_ref=zsend.at[k - 1, ch], dst_ref=zrec.at[k - 1, ch],
                send_sem=z_s.at[k - 1, ch], recv_sem=z_r.at[k - 1, ch],
                device_id=(d, to), device_id_type=MESH)
            copy.start()
            zcopies[k, ch] = copy

    part = pl.ds(pl.multiple_of(s * tt, 8), tt)
    score = jnp.zeros((tt, 1), F32)
    for ch in range(nch):
        total = jnp.concatenate([acc[ch, 0, part, :], acc[ch, 1, part, :]], axis=0)
        for k in range(1, nt):
            zcopies[k, ch].wait_recv()
            total = total + zrec[k - 1, ch].astype(F32)
        out_ref[:, ch * cw:(ch + 1) * cw] = total[:tt].astype(BF16)
        gap = total[tt:]
        score = score + jnp.sum(gap * gap, axis=1, keepdims=True)
    srec[0] = jnp.broadcast_to(score / SCORE_DIVISOR, (tt, HB))
    scopies = []
    for k in range(1, ndp):
        copy = pltpu.make_async_remote_copy(
            src_ref=srec.at[0], dst_ref=srec.at[k], send_sem=s_s.at[k], recv_sem=s_r.at[k],
            device_id=(lax.rem(d + k, ndp), s), device_id_type=MESH)
        copy.start()
        scopies.append(copy)
    for copy in scopies:
        copy.wait_recv()
    total = jnp.zeros((tt, HB), F32)
    for j in range(ndp):
        total = total + srec[lax.rem(d - j + ndp, ndp)]
    score_ref[...] = total

    for copy in (xcopies + wincopies + wcopies + list(pcopies.values()) + list(zcopies.values())
                 + scopies):
        copy.wait_send()


def local(ndp, nt, activations, weight_codes, scale_index, scale_table, bit_widths):
    z = sizes(ndp, nt, activations.shape, weight_codes.shape)
    chips, cw, nch, tt, rp = z["chips"], z["cw"], z["nch"], z["tt"], z["rp"]
    tp, nb, nblk, cols, tokens = z["tp"], z["nb"], z["nblk"], z["cols"], z["tokens"]
    vmem = pl.BlockSpec(memory_space=pltpu.VMEM)
    dma = lambda *shape: pltpu.SemaphoreType.DMA(shape)
    others = max(chips - 1, 1)
    ties = max(nt - 1, 1)
    out, scores = pl.pallas_call(
        functools.partial(kernel, z),
        out_shape=(
            jax.ShapeDtypeStruct((tt, cols), BF16),
            jax.ShapeDtypeStruct((tt, HB), F32),
        ),
        in_specs=[vmem, pl.BlockSpec(memory_space=pl.ANY), vmem,
                  pl.BlockSpec(memory_space=pltpu.SMEM), vmem, vmem],
        out_specs=(vmem, vmem),
        scratch_shapes=[
            pltpu.VMEM(weight_codes.shape, I32),
            pltpu.VMEM((nt, nblk * tp, HB), BF16),
            pltpu.VMEM((nblk * tp, HB), BF16),
            pltpu.VMEM((ndp, nb * tp, HB), BF16),
            pltpu.VMEM((ndp * tp, nb * HB), BF16),
            pltpu.VMEM((2, tokens, rp), BF16),
            pltpu.VMEM((2, chips, 2, rp, cols), BF16),
            pltpu.VMEM((chips, 2, rp, cols), BF16),
            pltpu.VMEM((others, nch, 2, tokens, cw), BF16),
            pltpu.VMEM((others, nch, 2, tokens, cw), BF16),
            pltpu.VMEM((nch, 2, tokens, cw), F32),
            pltpu.VMEM((ties, nch, 2 * tt, cw), BF16),
            pltpu.VMEM((ties, nch, 2 * tt, cw), BF16),
            pltpu.VMEM((ndp, tt, HB), F32),
            dma(chips), dma(nt), dma(nt), dma(ndp), dma(ndp), dma(chips), dma(chips),
            dma(others, nch), dma(others, nch), dma(ties, nch), dma(ties, nch),
            dma(ndp), dma(ndp),
        ],
        compiler_params=pltpu.CompilerParams(
            collective_id=0, has_side_effects=True, vmem_limit_bytes=56 * 2 ** 20),
    )(activations, weight_codes, scale_index, scale_table, bit_widths[0],
      jnp.asarray(sylvester(HB), BF16))
    return out, scores[:, 0][None]


def solution(mesh):
    in_specs = (
        P("dp", "tensor"),
        P(("tensor", "dp"), None),
        P(("tensor", "dp"), None),
        P(),
        P(None, ("tensor", "dp"), None),
    )
    out_specs = (P("tensor", "dp"), P(None, "tensor"))
    body = functools.partial(local, mesh.shape["dp"], mesh.shape["tensor"])
    return jax.shard_map(body, mesh=mesh, in_specs=in_specs, out_specs=out_specs, check_vma=False)
```

```python
import functools
import math

import jax
import jax.numpy as jnp
import numpy as np
from jax import lax
from jax.experimental import pallas as pl
from jax.experimental.pallas import tpu as pltpu
from jax.sharding import PartitionSpec as P

HB = 128
SCORE_DIVISOR = 512.0
MESH = pl.DeviceIdType.MESH
BF16, F32, I32 = jnp.bfloat16, jnp.float32, jnp.int32


def sylvester(order):
    bits = np.arange(order)[:, None] & np.arange(order)[None, :]
    parity = np.zeros((order, order), np.int32)
    for shift in range(order.bit_length()):
        parity += (bits >> shift) & 1
    return (1 - 2 * (parity % 2)).astype(np.float32)


def up16(count):
    return -(-count // 16) * 16


def sizes(ndp, nt, act_shape, code_shape):
    tl, width = act_shape
    rows, model = code_shape
    z = dict(ndp=ndp, nt=nt, chips=ndp // 2, tl=tl, nblk=width // HB, rows=rows)
    z["rp"] = up16(rows)
    z["cols"] = model // ndp
    z["tokens"] = tl * ndp
    z["tt"] = z["tokens"] // nt
    pair = 2 * rows
    spans = [(c * pair + pair - 1) // HB - c * pair // HB + 1 for c in range(z["chips"])]
    z["nb"] = min(max(spans), z["nblk"])
    z["cw"] = 256 if z["cols"] % 256 == 0 else z["cols"]
    z["nch"] = z["cols"] // z["cw"]
    z["xr"] = up16(z["nblk"] * tl)
    z["wr"] = up16(z["nb"] * tl)
    z["starts"] = [min(c * pair // HB, z["nblk"] - z["nb"]) for c in range(z["chips"])]
    return z


def kernel(z, act_ref, code_hbm, index_ref, table_ref, bits_ref, had_ref, out_ref, score_ref,
           codes, xs, fat, wsend, win, wpad, shifts, lhs, weights, wrecv, psend, prec, acc, zsend, zrec, srec,
           code_sem, xs_s, xs_r, win_s, win_r, w_s, w_r, p_s, p_r, z_s, z_r, s_s, s_r):
    ndp, nt, chips = z["ndp"], z["nt"], z["chips"]
    tl, nblk, nb = z["tl"], z["nblk"], z["nb"]
    rows, rp, cols, tokens, tt = z["rows"], z["rp"], z["cols"], z["tokens"], z["tt"]
    cw, nch, xr, wr, starts = z["cw"], z["nch"], z["xr"], z["wr"], z["starts"]
    d = lax.axis_index("dp")
    s = lax.axis_index("tensor")
    chip, core = d // 2, d % 2

    loads = []
    for k in range(chips):
        span = pl.ds(pl.multiple_of(lax.rem(chip + k, chips) * (2 * cols), 128), 2 * cols)
        loads.append(pltpu.make_async_copy(code_hbm.at[:, span], codes.at[k], code_sem.at[k]))
    for k in [*range(1, chips), 0]:
        loads[k].start()

    barrier = pltpu.get_barrier_semaphore()
    for k in range(1, ndp):
        pl.semaphore_signal(barrier, inc=1, device_id=(lax.rem(d + k, ndp), s), device_id_type=MESH)
    for k in range(1, nt):
        pl.semaphore_signal(barrier, inc=1, device_id=(d, lax.rem(s + k, nt)), device_id_type=MESH)

    act = act_ref[...].astype(F32)
    fat[nblk * tl:, :] = jnp.zeros((xr + wr - nblk * tl, HB), F32)
    for n in range(nblk):
        fat[n * tl:(n + 1) * tl, :] = act[:, n * HB:(n + 1) * HB]
    xs[0] = fat[0:xr, :].astype(BF16)

    pl.semaphore_wait(barrier, ndp - 1 + nt - 1)

    xcopies = []
    for k in range(1, nt):
        copy = pltpu.make_async_remote_copy(
            src_ref=xs.at[0], dst_ref=xs.at[k], send_sem=xs_s.at[k], recv_sem=xs_r.at[k],
            device_id=(d, lax.rem(s + k, nt)), device_id_type=MESH)
        copy.start()
        xcopies.append(copy)

    f_id = lax.broadcasted_iota(I32, (nb * HB, rp), 0)
    r_id = lax.broadcasted_iota(I32, (nb * HB, rp), 1)
    mine = jnp.minimum(chip * (2 * rows) // HB, nblk - nb)
    offset = chip * (2 * rows) - mine * HB
    for half in range(2):
        owner = lax.rem(core + half, 2)
        shift = (f_id == offset + owner * rows + r_id) & (r_id < rows)
        shifts[half] = shift.astype(F32).astype(BF16)

    groups = cols // HB
    lanes = index_ref.shape[0]

    def columns(rowwise):
        wide = jnp.concatenate([rowwise] * max(HB // lanes, 1), axis=0)
        wide = jnp.transpose(wide)
        turn = lax.rem(wide.shape[1] - lax.rem(chip * (2 * groups), wide.shape[1]), wide.shape[1])
        return pltpu.roll(wide, turn, 1)

    index = index_ref[...]
    scales = jnp.zeros(index.shape, F32)
    for i in range(table_ref.shape[0]):
        scales = jnp.where(index == i, table_ref[i], scales)
    bits = bits_ref[...]
    scales = columns(scales)
    step = columns(jnp.where(bits == 2, 4, jnp.where(bits == 3, 2, 1)).astype(I32))

    if rp != rows:
        weights[...] = jnp.zeros(weights.shape, BF16)
    wcopies = {}

    def dequantize(rel):
        loads[rel].wait()
        for half in range(2):
            away = lax.rem(core + half, 2)
            for g in range(groups):
                at = half * groups + g
                gg = (rel * 2 * groups + at) % lanes
                c = codes[rel, :, at * HB:(at + 1) * HB]
                sc = scales[:, gg:gg + 1]
                st = step[:, gg:gg + 1]
                base = ((c - 8).astype(F32) * sc).astype(BF16)
                cand = (((c & -st) + ((st >> 1) - 8)).astype(F32) * sc).astype(BF16)
                gap = (cand.astype(F32) - base.astype(F32)).astype(BF16)
                weights[away, rel, 0, 0:rows, g * HB:(g + 1) * HB] = base
                weights[away, rel, 1, 0:rows, g * HB:(g + 1) * HB] = gap
        copy = pltpu.make_async_remote_copy(
            src_ref=weights.at[1, rel], dst_ref=wrecv.at[rel], send_sem=w_s.at[rel],
            recv_sem=w_r.at[rel], device_id=(chip * 2 + 1 - core, s), device_id_type=MESH)
        copy.start()
        wcopies[rel] = copy

    def rotate():
        total = jnp.zeros((xr, HB), F32)
        for k in range(nt):
            if k:
                xcopies[k - 1].wait_recv()
            src = lax.rem(s - k + nt, nt)
            parity = 0
            for b in range(max(nt.bit_length() - 1, 0)):
                parity = parity + (src // 2 ** b % 2) * (s // 2 ** b % 2)
            sign = (1 - 2 * (parity % 2)).astype(F32)
            total = total + sign * jnp.dot(xs[k], had_ref[...], preferred_element_type=F32)
        fat[0:xr, :] = total * (1.0 / math.sqrt(HB * nt))
        for c in range(chips):
            wsend[c] = fat[starts[c] * tl:starts[c] * tl + wr, :].astype(BF16)
        copies = []
        for k in range(1, ndp):
            to = lax.rem(d + k, ndp)
            copy = pltpu.make_async_remote_copy(
                src_ref=wsend.at[to // 2], dst_ref=win.at[d], send_sem=win_s.at[k],
                recv_sem=win_r.at[k], device_id=(to, s), device_id_type=MESH)
            copy.start()
            copies.append(copy)
        win[d] = wsend[chip]
        return copies

    def product(k, kind, ch):
        span = slice(ch * cw, (ch + 1) * cw)
        return (jnp.dot(lhs[0], weights[0, k, kind, :, span], preferred_element_type=F32)
                + jnp.dot(lhs[1], wrecv[k, kind, :, span], preferred_element_type=F32))

    early = list(range(1, 1 + (chips - 1) // 3))
    late = list(range(1 + (chips - 1) // 3, chips))
    for k in early:
        dequantize(k)
    wincopies = rotate()
    for k in late:
        dequantize(k)

    for copy in wincopies:
        copy.wait_recv()
    for j in range(ndp):
        got = win[j].astype(F32)
        for n in range(nb):
            wpad[j * tl:(j + 1) * tl, n * HB:(n + 1) * HB] = got[n * tl:(n + 1) * tl, :]
    ordered = wpad[...].astype(BF16)
    for half in range(2):
        lhs[half] = jnp.dot(ordered, shifts[half], preferred_element_type=F32).astype(BF16)

    pcopies = {}

    def partial(k, ch):
        for kind in range(2):
            psend[k - 1, ch, kind] = product(k, kind, ch).astype(BF16)
        copy = pltpu.make_async_remote_copy(
            src_ref=psend.at[k - 1, ch], dst_ref=prec.at[k - 1, ch],
            send_sem=p_s.at[k - 1, ch], recv_sem=p_r.at[k - 1, ch],
            device_id=(lax.rem(chip + k, chips) * 2 + core, s), device_id_type=MESH)
        copy.start()
        pcopies[k, ch] = copy

    for k in early:
        wcopies[k].wait_recv()
        for ch in range(nch):
            partial(k, ch)
    for k in late:
        wcopies[k].wait_recv()
    for ch in range(nch):
        for k in late:
            partial(k, ch)
    dequantize(0)
    wcopies[0].wait_recv()
    for ch in range(nch):
        for kind in range(2):
            acc[ch, kind] = product(0, kind, ch)

    zcopies = {}
    for ch in range(nch):
        for k in range(1, chips):
            pcopies[k, ch].wait_recv()
        for kind in range(2):
            total = acc[ch, kind]
            for k in range(1, chips):
                total = total + prec[k - 1, ch, kind].astype(F32)
            acc[ch, kind] = total
        for k in range(1, nt):
            to = lax.rem(s + k, nt)
            part = pl.ds(pl.multiple_of(to * tt, 8), tt)
            zsend[k - 1, ch] = jnp.concatenate(
                [acc[ch, 0, part, :], acc[ch, 1, part, :]], axis=0).astype(BF16)
            copy = pltpu.make_async_remote_copy(
                src_ref=zsend.at[k - 1, ch], dst_ref=zrec.at[k - 1, ch],
                send_sem=z_s.at[k - 1, ch], recv_sem=z_r.at[k - 1, ch],
                device_id=(d, to), device_id_type=MESH)
            copy.start()
            zcopies[k, ch] = copy

    part = pl.ds(pl.multiple_of(s * tt, 8), tt)
    score = jnp.zeros((tt, 1), F32)
    for ch in range(nch):
        total = jnp.concatenate([acc[ch, 0, part, :], acc[ch, 1, part, :]], axis=0)
        for k in range(1, nt):
            zcopies[k, ch].wait_recv()
            total = total + zrec[k - 1, ch].astype(F32)
        out_ref[:, ch * cw:(ch + 1) * cw] = total[:tt].astype(BF16)
        gap = total[tt:]
        score = score + jnp.sum(gap * gap, axis=1, keepdims=True)
    srec[0] = jnp.broadcast_to(score / SCORE_DIVISOR, (tt, HB))
    scopies = []
    for k in range(1, ndp):
        copy = pltpu.make_async_remote_copy(
            src_ref=srec.at[0], dst_ref=srec.at[k], send_sem=s_s.at[k], recv_sem=s_r.at[k],
            device_id=(lax.rem(d + k, ndp), s), device_id_type=MESH)
        copy.start()
        scopies.append(copy)
    for copy in scopies:
        copy.wait_recv()
    total = jnp.zeros((tt, HB), F32)
    for j in range(ndp):
        total = total + srec[lax.rem(d - j + ndp, ndp)]
    score_ref[...] = total

    for copy in (xcopies + wincopies + list(wcopies.values()) + list(pcopies.values()) + list(zcopies.values())
                 + scopies):
        copy.wait_send()


def local(ndp, nt, activations, weight_codes, scale_index, scale_table, bit_widths):
    z = sizes(ndp, nt, activations.shape, weight_codes.shape)
    chips, cw, nch, tt, rp = z["chips"], z["cw"], z["nch"], z["tt"], z["rp"]
    nb, cols, tokens = z["nb"], z["cols"], z["tokens"]
    vmem = pl.BlockSpec(memory_space=pltpu.VMEM)
    dma = lambda *shape: pltpu.SemaphoreType.DMA(shape)
    others = max(chips - 1, 1)
    ties = max(nt - 1, 1)
    out, scores = pl.pallas_call(
        functools.partial(kernel, z),
        out_shape=(
            jax.ShapeDtypeStruct((tt, cols), BF16),
            jax.ShapeDtypeStruct((tt, HB), F32),
        ),
        in_specs=[vmem, pl.BlockSpec(memory_space=pl.ANY), vmem,
                  pl.BlockSpec(memory_space=pltpu.SMEM), vmem, vmem],
        out_specs=(vmem, vmem),
        scratch_shapes=[
            pltpu.VMEM((chips, z["rows"], 2 * cols), I32),
            pltpu.VMEM((nt, z["xr"], HB), BF16),
            pltpu.VMEM((z["xr"] + z["wr"], HB), F32),
            pltpu.VMEM((chips, z["wr"], HB), BF16),
            pltpu.VMEM((ndp, z["wr"], HB), BF16),
            pltpu.VMEM((tokens, nb * HB), F32),
            pltpu.VMEM((2, nb * HB, rp), BF16),
            pltpu.VMEM((2, tokens, rp), BF16),
            pltpu.VMEM((2, chips, 2, rp, cols), BF16),
            pltpu.VMEM((chips, 2, rp, cols), BF16),
            pltpu.VMEM((others, nch, 2, tokens, cw), BF16),
            pltpu.VMEM((others, nch, 2, tokens, cw), BF16),
            pltpu.VMEM((nch, 2, tokens, cw), F32),
            pltpu.VMEM((ties, nch, 2 * tt, cw), BF16),
            pltpu.VMEM((ties, nch, 2 * tt, cw), BF16),
            pltpu.VMEM((ndp, tt, HB), F32),
            dma(chips), dma(nt), dma(nt), dma(ndp), dma(ndp), dma(chips), dma(chips),
            dma(others, nch), dma(others, nch), dma(ties, nch), dma(ties, nch),
            dma(ndp), dma(ndp),
        ],
        compiler_params=pltpu.CompilerParams(
            collective_id=0, has_side_effects=True, vmem_limit_bytes=56 * 2 ** 20),
    )(activations, weight_codes, scale_index.T, scale_table, bit_widths[0].T,
      jnp.asarray(sylvester(HB), BF16))
    return out, scores[:, 0][None]


def solution(mesh):
    in_specs = (
        P("dp", "tensor"),
        P(("tensor", "dp"), None),
        P(("tensor", "dp"), None),
        P(),
        P(None, ("tensor", "dp"), None),
    )
    out_specs = (P("tensor", "dp"), P(None, "tensor"))
    body = functools.partial(local, mesh.shape["dp"], mesh.shape["tensor"])
    return jax.shard_map(body, mesh=mesh, in_specs=in_specs, out_specs=out_specs, check_vma=False)
```

```python
import functools
import math

import jax
import jax.numpy as jnp
import numpy as np
from jax import lax
from jax.experimental import pallas as pl
from jax.experimental.pallas import tpu as pltpu
from jax.sharding import PartitionSpec as P

HB = 128
SCORE_DIVISOR = 512.0
MESH = pl.DeviceIdType.MESH
BF16, F32, I32 = jnp.bfloat16, jnp.float32, jnp.int32


def sylvester(order):
    bits = np.arange(order)[:, None] & np.arange(order)[None, :]
    parity = np.zeros((order, order), np.int32)
    for shift in range(order.bit_length()):
        parity += (bits >> shift) & 1
    return (1 - 2 * (parity % 2)).astype(np.float32)


def up16(count):
    return -(-count // 16) * 16


def sizes(ndp, nt, act_shape, code_shape):
    tl, width = act_shape
    rows, model = code_shape
    z = dict(ndp=ndp, nt=nt, chips=ndp // 2, tl=tl, nblk=width // HB, rows=rows)
    z["rp"] = up16(rows)
    z["cols"] = model // ndp
    z["tokens"] = tl * ndp
    z["tt"] = z["tokens"] // nt
    pair = 2 * rows
    spans = [(c * pair + pair - 1) // HB - c * pair // HB + 1 for c in range(z["chips"])]
    z["nb"] = min(max(spans), z["nblk"])
    z["cw"] = 256 if z["cols"] % 256 == 0 else z["cols"]
    z["nch"] = z["cols"] // z["cw"]
    z["tree"] = z["chips"] == 4 and z["tokens"] % 32 == 0
    z["xr"] = up16(z["nblk"] * tl)
    z["wr"] = up16(z["nb"] * tl)
    z["starts"] = [min(c * pair // HB, z["nblk"] - z["nb"]) for c in range(z["chips"])]
    return z


def kernel(z, act_ref, code_hbm, index_ref, table_ref, bits_ref, had_ref, out_ref, score_ref,
           codes, xs, fat, wsend, win, wpad, shifts, lhs, weights, wrecv, psend, prec, keep, acc, zsend, zrec, srec,
           code_sem, xs_s, xs_r, win_s, win_r, w_s, w_r, p_s, p_r, z_s, z_r, s_s, s_r):
    ndp, nt, chips = z["ndp"], z["nt"], z["chips"]
    tl, nblk, nb = z["tl"], z["nblk"], z["nb"]
    rows, rp, cols, tokens, tt = z["rows"], z["rp"], z["cols"], z["tokens"], z["tt"]
    cw, nch, xr, wr, starts = z["cw"], z["nch"], z["xr"], z["wr"], z["starts"]
    d = lax.axis_index("dp")
    s = lax.axis_index("tensor")
    chip, core = d // 2, d % 2

    loads = []
    for k in range(chips):
        span = pl.ds(pl.multiple_of(lax.rem(chip + k, chips) * (2 * cols), 128), 2 * cols)
        loads.append(pltpu.make_async_copy(code_hbm.at[:, span], codes.at[k], code_sem.at[k]))
    for k in [*range(1, chips), 0]:
        loads[k].start()

    barrier = pltpu.get_barrier_semaphore()
    for k in range(1, ndp):
        pl.semaphore_signal(barrier, inc=1, device_id=(lax.rem(d + k, ndp), s), device_id_type=MESH)
    for k in range(1, nt):
        pl.semaphore_signal(barrier, inc=1, device_id=(d, lax.rem(s + k, nt)), device_id_type=MESH)

    act = act_ref[...].astype(F32)
    fat[nblk * tl:, :] = jnp.zeros((xr + wr - nblk * tl, HB), F32)
    for n in range(nblk):
        fat[n * tl:(n + 1) * tl, :] = act[:, n * HB:(n + 1) * HB]
    xs[0] = fat[0:xr, :].astype(BF16)

    pl.semaphore_wait(barrier, ndp - 1 + nt - 1)

    xcopies = []
    for k in range(1, nt):
        copy = pltpu.make_async_remote_copy(
            src_ref=xs.at[0], dst_ref=xs.at[k], send_sem=xs_s.at[k], recv_sem=xs_r.at[k],
            device_id=(d, lax.rem(s + k, nt)), device_id_type=MESH)
        copy.start()
        xcopies.append(copy)

    f_id = lax.broadcasted_iota(I32, (nb * HB, rp), 0)
    r_id = lax.broadcasted_iota(I32, (nb * HB, rp), 1)
    mine = jnp.minimum(chip * (2 * rows) // HB, nblk - nb)
    offset = chip * (2 * rows) - mine * HB
    for half in range(2):
        owner = lax.rem(core + half, 2)
        shift = (f_id == offset + owner * rows + r_id) & (r_id < rows)
        shifts[half] = shift.astype(F32).astype(BF16)

    groups = cols // HB
    lanes = index_ref.shape[0]

    def columns(rowwise):
        wide = jnp.concatenate([rowwise] * max(HB // lanes, 1), axis=0)
        wide = jnp.transpose(wide)
        turn = lax.rem(wide.shape[1] - lax.rem(chip * (2 * groups), wide.shape[1]), wide.shape[1])
        return pltpu.roll(wide, turn, 1)

    index = index_ref[...]
    scales = jnp.zeros(index.shape, F32)
    for i in range(table_ref.shape[0]):
        scales = jnp.where(index == i, table_ref[i], scales)
    bits = bits_ref[...]
    scales = columns(scales)
    step = columns(jnp.where(bits == 2, 4, jnp.where(bits == 3, 2, 1)).astype(I32))

    if rp != rows:
        weights[...] = jnp.zeros(weights.shape, BF16)
    wcopies = {}

    def dequantize(rel):
        loads[rel].wait()
        for half in range(2):
            away = lax.rem(core + half, 2)
            for g in range(groups):
                at = half * groups + g
                gg = (rel * 2 * groups + at) % lanes
                c = codes[rel, :, at * HB:(at + 1) * HB]
                sc = scales[:, gg:gg + 1]
                st = step[:, gg:gg + 1]
                base = ((c - 8).astype(F32) * sc).astype(BF16)
                cand = (((c & -st) + ((st >> 1) - 8)).astype(F32) * sc).astype(BF16)
                gap = (cand.astype(F32) - base.astype(F32)).astype(BF16)
                weights[away, rel, 0, 0:rows, g * HB:(g + 1) * HB] = base
                weights[away, rel, 1, 0:rows, g * HB:(g + 1) * HB] = gap
        copy = pltpu.make_async_remote_copy(
            src_ref=weights.at[1, rel], dst_ref=wrecv.at[rel], send_sem=w_s.at[rel],
            recv_sem=w_r.at[rel], device_id=(chip * 2 + 1 - core, s), device_id_type=MESH)
        copy.start()
        wcopies[rel] = copy

    def rotate():
        total = jnp.zeros((xr, HB), F32)
        for k in range(nt):
            if k:
                xcopies[k - 1].wait_recv()
            src = lax.rem(s - k + nt, nt)
            parity = 0
            for b in range(max(nt.bit_length() - 1, 0)):
                parity = parity + (src // 2 ** b % 2) * (s // 2 ** b % 2)
            sign = (1 - 2 * (parity % 2)).astype(F32)
            total = total + sign * jnp.dot(xs[k], had_ref[...], preferred_element_type=F32)
        fat[0:xr, :] = total * (1.0 / math.sqrt(HB * nt))
        for c in range(chips):
            wsend[c] = fat[starts[c] * tl:starts[c] * tl + wr, :].astype(BF16)
        copies = []
        for k in range(1, ndp):
            to = lax.rem(d + k, ndp)
            copy = pltpu.make_async_remote_copy(
                src_ref=wsend.at[to // 2], dst_ref=win.at[d], send_sem=win_s.at[k],
                recv_sem=win_r.at[k], device_id=(to, s), device_id_type=MESH)
            copy.start()
            copies.append(copy)
        win[d] = wsend[chip]
        return copies

    def product(k, kind, ch):
        span = slice(ch * cw, (ch + 1) * cw)
        return (jnp.dot(lhs[0], weights[0, k, kind, :, span], preferred_element_type=F32)
                + jnp.dot(lhs[1], wrecv[k, kind, :, span], preferred_element_type=F32))

    early = list(range(1, 1 + (chips - 1) // 3))
    late = list(range(1 + (chips - 1) // 3, chips))
    if z["tree"]:
        late = late[::-1]
    for k in early:
        dequantize(k)
    wincopies = rotate()
    for k in late:
        dequantize(k)

    for copy in wincopies:
        copy.wait_recv()
    for j in range(ndp):
        got = win[j].astype(F32)
        for n in range(nb):
            wpad[j * tl:(j + 1) * tl, n * HB:(n + 1) * HB] = got[n * tl:(n + 1) * tl, :]
    ordered = wpad[...].astype(BF16)
    for half in range(2):
        lhs[half] = jnp.dot(ordered, shifts[half], preferred_element_type=F32).astype(BF16)

    pcopies = {}

    def partial(k, ch):
        for kind in range(2):
            psend[k - 1, ch, kind] = product(k, kind, ch).astype(BF16)
        copy = pltpu.make_async_remote_copy(
            src_ref=psend.at[k - 1, ch], dst_ref=prec.at[k - 1, ch],
            send_sem=p_s.at[k - 1, ch], recv_sem=p_r.at[k - 1, ch],
            device_id=(lax.rem(chip + k, chips) * 2 + core, s), device_id_type=MESH)
        copy.start()
        pcopies[k, ch] = copy

    half_tokens = tokens // 2
    odd = lax.rem(chip, 2)
    near = (chip + 1 - 2 * odd, lax.rem(chip + 2, chips))
    k_near = (1 + 2 * odd, 2)
    k_far = 3 - 2 * odd

    def ship(stage, h, ch, to):
        at = stage * 2 + h
        copy = pltpu.make_async_remote_copy(
            src_ref=psend.at[at, ch], dst_ref=prec.at[at, ch], send_sem=p_s.at[at, ch],
            recv_sem=p_r.at[at, ch], device_id=(to * 2 + core, s), device_id_type=MESH)
        copy.start()
        pcopies[at, ch] = copy

    if z["tree"]:
        wcopies[1].wait_recv()
        wcopies[3].wait_recv()
        for ch in range(nch):
            for kind in range(2):
                far = product(k_far, kind, ch).astype(BF16)
                psend[0, ch, kind] = far[:half_tokens]
                psend[1, ch, kind] = far[half_tokens:]
            for h in range(2):
                ship(0, h, ch, near[h])
        dequantize(0)
        wcopies[2].wait_recv()
        wcopies[0].wait_recv()
        for ch in range(nch):
            for h in range(2):
                for kind in range(2):
                    block = product(k_near[h], kind, ch)
                    first, second = block[:half_tokens], block[half_tokens:]
                    psend[2 + h, ch, kind] = (second if h else first).astype(BF16)
                    keep[1 - h, ch, kind] = first if h else second
                ship(1, h, ch, near[h])
            for h in range(2):
                pcopies[h, ch].wait_recv()
                for kind in range(2):
                    psend[4 + h, ch, kind] = (
                        keep[h, ch, kind] + prec[h, ch, kind].astype(F32)).astype(BF16)
                ship(2, h, ch, near[1 - h])
            for kind in range(2):
                acc[ch, kind] = product(0, kind, ch)
    else:
        for k in early:
            wcopies[k].wait_recv()
            for ch in range(nch):
                partial(k, ch)
        for k in late:
            wcopies[k].wait_recv()
        for ch in range(nch):
            for k in late:
                partial(k, ch)
        dequantize(0)
        wcopies[0].wait_recv()
        for ch in range(nch):
            for kind in range(2):
                acc[ch, kind] = product(0, kind, ch)

    zcopies = {}
    for ch in range(nch):
        for (k, c), copy in pcopies.items():
            if c == ch and not (z["tree"] and k < 2):
                copy.wait_recv()
        for kind in range(2):
            if z["tree"]:
                for h in range(2):
                    span = slice(h * half_tokens, (h + 1) * half_tokens)
                    acc[ch, kind, span, :] = (acc[ch, kind, span, :]
                                              + prec[2 + h, ch, kind].astype(F32)
                                              + prec[4 + h, ch, kind].astype(F32))
            else:
                total = acc[ch, kind]
                for k in range(1, chips):
                    total = total + prec[k - 1, ch, kind].astype(F32)
                acc[ch, kind] = total
        for k in range(1, nt):
            to = lax.rem(s + k, nt)
            part = pl.ds(pl.multiple_of(to * tt, 8), tt)
            zsend[k - 1, ch] = jnp.concatenate(
                [acc[ch, 0, part, :], acc[ch, 1, part, :]], axis=0).astype(BF16)
            copy = pltpu.make_async_remote_copy(
                src_ref=zsend.at[k - 1, ch], dst_ref=zrec.at[k - 1, ch],
                send_sem=z_s.at[k - 1, ch], recv_sem=z_r.at[k - 1, ch],
                device_id=(d, to), device_id_type=MESH)
            copy.start()
            zcopies[k, ch] = copy

    part = pl.ds(pl.multiple_of(s * tt, 8), tt)
    score = jnp.zeros((tt, 1), F32)
    for ch in range(nch):
        total = jnp.concatenate([acc[ch, 0, part, :], acc[ch, 1, part, :]], axis=0)
        for k in range(1, nt):
            zcopies[k, ch].wait_recv()
            total = total + zrec[k - 1, ch].astype(F32)
        out_ref[:, ch * cw:(ch + 1) * cw] = total[:tt].astype(BF16)
        gap = total[tt:]
        score = score + jnp.sum(gap * gap, axis=1, keepdims=True)
    srec[0] = jnp.broadcast_to(score / SCORE_DIVISOR, (tt, HB))
    scopies = []
    for k in range(1, ndp):
        copy = pltpu.make_async_remote_copy(
            src_ref=srec.at[0], dst_ref=srec.at[k], send_sem=s_s.at[k], recv_sem=s_r.at[k],
            device_id=(lax.rem(d + k, ndp), s), device_id_type=MESH)
        copy.start()
        scopies.append(copy)
    for copy in scopies:
        copy.wait_recv()
    total = jnp.zeros((tt, HB), F32)
    for j in range(ndp):
        total = total + srec[lax.rem(d - j + ndp, ndp)]
    score_ref[...] = total

    for copy in (xcopies + wincopies + list(wcopies.values()) + list(pcopies.values()) + list(zcopies.values())
                 + scopies):
        copy.wait_send()


def local(ndp, nt, activations, weight_codes, scale_index, scale_table, bit_widths):
    z = sizes(ndp, nt, activations.shape, weight_codes.shape)
    chips, cw, nch, tt, rp = z["chips"], z["cw"], z["nch"], z["tt"], z["rp"]
    nb, cols, tokens = z["nb"], z["cols"], z["tokens"]
    vmem = pl.BlockSpec(memory_space=pltpu.VMEM)
    dma = lambda *shape: pltpu.SemaphoreType.DMA(shape)
    others, high = (6, tokens // 2) if z["tree"] else (max(chips - 1, 1), tokens)
    ties = max(nt - 1, 1)
    out, scores = pl.pallas_call(
        functools.partial(kernel, z),
        out_shape=(
            jax.ShapeDtypeStruct((tt, cols), BF16),
            jax.ShapeDtypeStruct((tt, HB), F32),
        ),
        in_specs=[vmem, pl.BlockSpec(memory_space=pl.ANY), vmem,
                  pl.BlockSpec(memory_space=pltpu.SMEM), vmem, vmem],
        out_specs=(vmem, vmem),
        scratch_shapes=[
            pltpu.VMEM((chips, z["rows"], 2 * cols), I32),
            pltpu.VMEM((nt, z["xr"], HB), BF16),
            pltpu.VMEM((z["xr"] + z["wr"], HB), F32),
            pltpu.VMEM((chips, z["wr"], HB), BF16),
            pltpu.VMEM((ndp, z["wr"], HB), BF16),
            pltpu.VMEM((tokens, nb * HB), F32),
            pltpu.VMEM((2, nb * HB, rp), BF16),
            pltpu.VMEM((2, tokens, rp), BF16),
            pltpu.VMEM((2, chips, 2, rp, cols), BF16),
            pltpu.VMEM((chips, 2, rp, cols), BF16),
            pltpu.VMEM((others, nch, 2, high, cw), BF16),
            pltpu.VMEM((others, nch, 2, high, cw), BF16),
            pltpu.VMEM((2, nch, 2, high, cw) if z["tree"] else (8, HB), F32),
            pltpu.VMEM((nch, 2, tokens, cw), F32),
            pltpu.VMEM((ties, nch, 2 * tt, cw), BF16),
            pltpu.VMEM((ties, nch, 2 * tt, cw), BF16),
            pltpu.VMEM((ndp, tt, HB), F32),
            dma(chips), dma(nt), dma(nt), dma(ndp), dma(ndp), dma(chips), dma(chips),
            dma(others, nch), dma(others, nch), dma(ties, nch), dma(ties, nch),
            dma(ndp), dma(ndp),
        ],
        compiler_params=pltpu.CompilerParams(
            collective_id=0, has_side_effects=True, vmem_limit_bytes=56 * 2 ** 20),
    )(activations, weight_codes, scale_index.T, scale_table, bit_widths[0].T,
      jnp.asarray(sylvester(HB), BF16))
    return out, scores[:, 0][None]


def solution(mesh):
    in_specs = (
        P("dp", "tensor"),
        P(("tensor", "dp"), None),
        P(("tensor", "dp"), None),
        P(),
        P(None, ("tensor", "dp"), None),
    )
    out_specs = (P("tensor", "dp"), P(None, "tensor"))
    body = functools.partial(local, mesh.shape["dp"], mesh.shape["tensor"])
    return jax.shard_map(body, mesh=mesh, in_specs=in_specs, out_specs=out_specs, check_vma=False)
```

```python
import functools
import math

import jax
import jax.numpy as jnp
import numpy as np
from jax import lax
from jax.experimental import pallas as pl
from jax.experimental.pallas import tpu as pltpu
from jax.sharding import PartitionSpec as P

HB = 128
SCORE_DIVISOR = 512.0
MESH = pl.DeviceIdType.MESH
BF16, F32, I32 = jnp.bfloat16, jnp.float32, jnp.int32


def sylvester(order):
    bits = np.arange(order)[:, None] & np.arange(order)[None, :]
    parity = np.zeros((order, order), np.int32)
    for shift in range(order.bit_length()):
        parity += (bits >> shift) & 1
    return (1 - 2 * (parity % 2)).astype(np.float32)


def up16(count):
    return -(-count // 16) * 16


def sizes(ndp, nt, act_shape, code_shape):
    tl, width = act_shape
    rows, model = code_shape
    z = dict(ndp=ndp, nt=nt, chips=ndp // 2, tl=tl, nblk=width // HB, rows=rows)
    z["rp"] = up16(rows)
    z["cols"] = model // ndp
    z["tokens"] = tl * ndp
    z["tt"] = z["tokens"] // nt
    pair = 2 * rows
    spans = [(c * pair + pair - 1) // HB - c * pair // HB + 1 for c in range(z["chips"])]
    z["nb"] = min(max(spans), z["nblk"])
    z["cw"] = 256 if z["cols"] % 256 == 0 else z["cols"]
    z["nch"] = z["cols"] // z["cw"]
    z["tree"] = z["chips"] == 4 and z["tokens"] % 32 == 0
    z["xr"] = up16(z["nblk"] * tl)
    z["wr"] = up16(z["nb"] * tl)
    z["starts"] = [min(c * pair // HB, z["nblk"] - z["nb"]) for c in range(z["chips"])]
    return z


def kernel(z, act_ref, code_hbm, index_ref, table_ref, bits_ref, had_ref, out_ref, score_ref,
           codes, xs, fat, wsend, win, wpad, shifts, lhs, weights, wrecv, psend, prec, keep, acc, zsend, zrec, srec,
           code_sem, xs_s, xs_r, win_s, win_r, w_s, w_r, p_s, p_r, z_s, z_r, s_s, s_r):
    ndp, nt, chips = z["ndp"], z["nt"], z["chips"]
    tl, nblk, nb = z["tl"], z["nblk"], z["nb"]
    rows, rp, cols, tokens, tt = z["rows"], z["rp"], z["cols"], z["tokens"], z["tt"]
    cw, nch, xr, wr, starts = z["cw"], z["nch"], z["xr"], z["wr"], z["starts"]
    d = lax.axis_index("dp")
    s = lax.axis_index("tensor")
    chip, core = d // 2, d % 2

    loads = []
    for k in range(chips):
        span = pl.ds(pl.multiple_of(lax.rem(chip + k, chips) * (2 * cols), 128), 2 * cols)
        loads.append(pltpu.make_async_copy(code_hbm.at[:, span], codes.at[k], code_sem.at[k]))
    for k in [*range(1, chips), 0]:
        loads[k].start()

    barrier = pltpu.get_barrier_semaphore()
    for k in range(1, ndp):
        pl.semaphore_signal(barrier, inc=1, device_id=(lax.rem(d + k, ndp), s), device_id_type=MESH)
    for k in range(1, nt):
        pl.semaphore_signal(barrier, inc=1, device_id=(d, lax.rem(s + k, nt)), device_id_type=MESH)

    act = act_ref[...].astype(F32)
    fat[nblk * tl:, :] = jnp.zeros((xr + wr - nblk * tl, HB), F32)
    for n in range(nblk):
        fat[n * tl:(n + 1) * tl, :] = act[:, n * HB:(n + 1) * HB]
    xs[0] = fat[0:xr, :].astype(BF16)

    pl.semaphore_wait(barrier, ndp - 1 + nt - 1)

    xcopies = []
    for k in range(1, nt):
        copy = pltpu.make_async_remote_copy(
            src_ref=xs.at[0], dst_ref=xs.at[k], send_sem=xs_s.at[k], recv_sem=xs_r.at[k],
            device_id=(d, lax.rem(s + k, nt)), device_id_type=MESH)
        copy.start()
        xcopies.append(copy)

    f_id = lax.broadcasted_iota(I32, (nb * HB, rp), 0)
    r_id = lax.broadcasted_iota(I32, (nb * HB, rp), 1)
    mine = jnp.minimum(chip * (2 * rows) // HB, nblk - nb)
    offset = chip * (2 * rows) - mine * HB
    for half in range(2):
        owner = lax.rem(core + half, 2)
        shift = (f_id == offset + owner * rows + r_id) & (r_id < rows)
        shifts[half] = shift.astype(F32).astype(BF16)

    groups = cols // HB
    lanes = index_ref.shape[0]

    def columns(rowwise):
        wide = jnp.concatenate([rowwise] * max(HB // lanes, 1), axis=0)
        wide = jnp.transpose(wide)
        turn = lax.rem(wide.shape[1] - lax.rem(chip * (2 * groups), wide.shape[1]), wide.shape[1])
        return pltpu.roll(wide, turn, 1)

    index = index_ref[...]
    scales = jnp.zeros(index.shape, F32)
    for i in range(table_ref.shape[0]):
        scales = jnp.where(index == i, table_ref[i], scales)
    bits = bits_ref[...]
    scales = columns(scales)
    step = columns(jnp.where(bits == 2, 4, jnp.where(bits == 3, 2, 1)).astype(I32))

    if rp != rows:
        weights[...] = jnp.zeros(weights.shape, BF16)
    wcopies = {}

    def dequantize(rel):
        loads[rel].wait()
        for half in range(2):
            away = lax.rem(core + half, 2)
            for g in range(groups):
                at = half * groups + g
                gg = (rel * 2 * groups + at) % lanes
                c = codes[rel, :, at * HB:(at + 1) * HB]
                sc = scales[:, gg:gg + 1]
                st = step[:, gg:gg + 1]
                base = ((c - 8).astype(F32) * sc).astype(BF16)
                cand = (((c & -st) + ((st >> 1) - 8)).astype(F32) * sc).astype(BF16)
                gap = (cand.astype(F32) - base.astype(F32)).astype(BF16)
                weights[away, rel, 0, 0:rows, g * HB:(g + 1) * HB] = base
                weights[away, rel, 1, 0:rows, g * HB:(g + 1) * HB] = gap
        copy = pltpu.make_async_remote_copy(
            src_ref=weights.at[1, rel], dst_ref=wrecv.at[rel], send_sem=w_s.at[rel],
            recv_sem=w_r.at[rel], device_id=(chip * 2 + 1 - core, s), device_id_type=MESH)
        copy.start()
        wcopies[rel] = copy

    def rotate():
        total = jnp.zeros((xr, HB), F32)
        for k in range(nt):
            if k:
                xcopies[k - 1].wait_recv()
            src = lax.rem(s - k + nt, nt)
            parity = 0
            for b in range(max(nt.bit_length() - 1, 0)):
                parity = parity + (src // 2 ** b % 2) * (s // 2 ** b % 2)
            sign = (1 - 2 * (parity % 2)).astype(F32)
            total = total + sign * jnp.dot(xs[k], had_ref[...], preferred_element_type=F32)
        fat[0:xr, :] = total * (1.0 / math.sqrt(HB * nt))
        for c in range(chips):
            wsend[c] = fat[starts[c] * tl:starts[c] * tl + wr, :].astype(BF16)
        copies = []
        for k in range(1, ndp):
            to = lax.rem(d + k, ndp)
            copy = pltpu.make_async_remote_copy(
                src_ref=wsend.at[to // 2], dst_ref=win.at[d], send_sem=win_s.at[k],
                recv_sem=win_r.at[k], device_id=(to, s), device_id_type=MESH)
            copy.start()
            copies.append(copy)
        win[d] = wsend[chip]
        return copies

    def product(k, kind, ch):
        span = slice(ch * cw, (ch + 1) * cw)
        return (jnp.dot(lhs[0], weights[0, k, kind, :, span], preferred_element_type=F32)
                + jnp.dot(lhs[1], wrecv[k, kind, :, span], preferred_element_type=F32))

    early = list(range(1, 1 + (chips - 1) // 3))
    late = list(range(1 + (chips - 1) // 3, chips))
    if z["tree"]:
        late = [3]
    for k in early:
        dequantize(k)
    wincopies = rotate()
    for k in late:
        dequantize(k)

    for copy in wincopies:
        copy.wait_recv()
    for j in range(ndp):
        got = win[j].astype(F32)
        for n in range(nb):
            wpad[j * tl:(j + 1) * tl, n * HB:(n + 1) * HB] = got[n * tl:(n + 1) * tl, :]
    ordered = wpad[...].astype(BF16)
    for half in range(2):
        lhs[half] = jnp.dot(ordered, shifts[half], preferred_element_type=F32).astype(BF16)

    pcopies = {}

    def partial(k, ch):
        for kind in range(2):
            psend[k - 1, ch, kind] = product(k, kind, ch).astype(BF16)
        copy = pltpu.make_async_remote_copy(
            src_ref=psend.at[k - 1, ch], dst_ref=prec.at[k - 1, ch],
            send_sem=p_s.at[k - 1, ch], recv_sem=p_r.at[k - 1, ch],
            device_id=(lax.rem(chip + k, chips) * 2 + core, s), device_id_type=MESH)
        copy.start()
        pcopies[k, ch] = copy

    half_tokens = tokens // 2
    odd = lax.rem(chip, 2)
    near = (chip + 1 - 2 * odd, lax.rem(chip + 2, chips))
    k_near = (1 + 2 * odd, 2)
    k_far = 3 - 2 * odd

    def ship(stage, h, ch, to):
        at = stage * 2 + h
        copy = pltpu.make_async_remote_copy(
            src_ref=psend.at[at, ch], dst_ref=prec.at[at, ch], send_sem=p_s.at[at, ch],
            recv_sem=p_r.at[at, ch], device_id=(to * 2 + core, s), device_id_type=MESH)
        copy.start()
        pcopies[at, ch] = copy

    if z["tree"]:
        wcopies[1].wait_recv()
        wcopies[3].wait_recv()
        for ch in range(nch):
            for kind in range(2):
                far = product(k_far, kind, ch).astype(BF16)
                psend[0, ch, kind] = far[:half_tokens]
                psend[1, ch, kind] = far[half_tokens:]
            for h in range(2):
                ship(0, h, ch, near[h])
        dequantize(2)
        dequantize(0)
        wcopies[2].wait_recv()
        wcopies[0].wait_recv()
        for ch in range(nch):
            for h in range(2):
                for kind in range(2):
                    block = product(k_near[h], kind, ch)
                    first, second = block[:half_tokens], block[half_tokens:]
                    psend[2 + h, ch, kind] = (second if h else first).astype(BF16)
                    keep[1 - h, ch, kind] = first if h else second
                ship(1, h, ch, near[h])
            for h in range(2):
                pcopies[h, ch].wait_recv()
                for kind in range(2):
                    psend[4 + h, ch, kind] = (
                        keep[h, ch, kind] + prec[h, ch, kind].astype(F32)).astype(BF16)
                ship(2, h, ch, near[1 - h])
            for kind in range(2):
                acc[ch, kind] = product(0, kind, ch)
    else:
        for k in early:
            wcopies[k].wait_recv()
            for ch in range(nch):
                partial(k, ch)
        for k in late:
            wcopies[k].wait_recv()
        for ch in range(nch):
            for k in late:
                partial(k, ch)
        dequantize(0)
        wcopies[0].wait_recv()
        for ch in range(nch):
            for kind in range(2):
                acc[ch, kind] = product(0, kind, ch)

    zcopies = {}
    for ch in range(nch):
        for (k, c), copy in pcopies.items():
            if c == ch and not (z["tree"] and k < 2):
                copy.wait_recv()
        for kind in range(2):
            if z["tree"]:
                for h in range(2):
                    span = slice(h * half_tokens, (h + 1) * half_tokens)
                    acc[ch, kind, span, :] = (acc[ch, kind, span, :]
                                              + prec[2 + h, ch, kind].astype(F32)
                                              + prec[4 + h, ch, kind].astype(F32))
            else:
                total = acc[ch, kind]
                for k in range(1, chips):
                    total = total + prec[k - 1, ch, kind].astype(F32)
                acc[ch, kind] = total
        for k in range(1, nt):
            to = lax.rem(s + k, nt)
            part = pl.ds(pl.multiple_of(to * tt, 8), tt)
            zsend[k - 1, ch] = jnp.concatenate(
                [acc[ch, 0, part, :], acc[ch, 1, part, :]], axis=0).astype(BF16)
            copy = pltpu.make_async_remote_copy(
                src_ref=zsend.at[k - 1, ch], dst_ref=zrec.at[k - 1, ch],
                send_sem=z_s.at[k - 1, ch], recv_sem=z_r.at[k - 1, ch],
                device_id=(d, to), device_id_type=MESH)
            copy.start()
            zcopies[k, ch] = copy

    part = pl.ds(pl.multiple_of(s * tt, 8), tt)
    score = jnp.zeros((tt, 1), F32)
    for ch in range(nch):
        total = jnp.concatenate([acc[ch, 0, part, :], acc[ch, 1, part, :]], axis=0)
        for k in range(1, nt):
            zcopies[k, ch].wait_recv()
            total = total + zrec[k - 1, ch].astype(F32)
        out_ref[:, ch * cw:(ch + 1) * cw] = total[:tt].astype(BF16)
        gap = total[tt:]
        score = score + jnp.sum(gap * gap, axis=1, keepdims=True)
    srec[0] = jnp.broadcast_to(score / SCORE_DIVISOR, (tt, HB))
    scopies = []
    for k in range(1, ndp):
        copy = pltpu.make_async_remote_copy(
            src_ref=srec.at[0], dst_ref=srec.at[k], send_sem=s_s.at[k], recv_sem=s_r.at[k],
            device_id=(lax.rem(d + k, ndp), s), device_id_type=MESH)
        copy.start()
        scopies.append(copy)
    for copy in scopies:
        copy.wait_recv()
    total = jnp.zeros((tt, HB), F32)
    for j in range(ndp):
        total = total + srec[lax.rem(d - j + ndp, ndp)]
    score_ref[...] = total

    for copy in (xcopies + wincopies + list(wcopies.values()) + list(pcopies.values()) + list(zcopies.values())
                 + scopies):
        copy.wait_send()


def local(ndp, nt, activations, weight_codes, scale_index, scale_table, bit_widths):
    z = sizes(ndp, nt, activations.shape, weight_codes.shape)
    chips, cw, nch, tt, rp = z["chips"], z["cw"], z["nch"], z["tt"], z["rp"]
    nb, cols, tokens = z["nb"], z["cols"], z["tokens"]
    vmem = pl.BlockSpec(memory_space=pltpu.VMEM)
    dma = lambda *shape: pltpu.SemaphoreType.DMA(shape)
    others, high = (6, tokens // 2) if z["tree"] else (max(chips - 1, 1), tokens)
    ties = max(nt - 1, 1)
    out, scores = pl.pallas_call(
        functools.partial(kernel, z),
        out_shape=(
            jax.ShapeDtypeStruct((tt, cols), BF16),
            jax.ShapeDtypeStruct((tt, HB), F32),
        ),
        in_specs=[vmem, pl.BlockSpec(memory_space=pl.ANY), vmem,
                  pl.BlockSpec(memory_space=pltpu.SMEM), vmem, vmem],
        out_specs=(vmem, vmem),
        scratch_shapes=[
            pltpu.VMEM((chips, z["rows"], 2 * cols), I32),
            pltpu.VMEM((nt, z["xr"], HB), BF16),
            pltpu.VMEM((z["xr"] + z["wr"], HB), F32),
            pltpu.VMEM((chips, z["wr"], HB), BF16),
            pltpu.VMEM((ndp, z["wr"], HB), BF16),
            pltpu.VMEM((tokens, nb * HB), F32),
            pltpu.VMEM((2, nb * HB, rp), BF16),
            pltpu.VMEM((2, tokens, rp), BF16),
            pltpu.VMEM((2, chips, 2, rp, cols), BF16),
            pltpu.VMEM((chips, 2, rp, cols), BF16),
            pltpu.VMEM((others, nch, 2, high, cw), BF16),
            pltpu.VMEM((others, nch, 2, high, cw), BF16),
            pltpu.VMEM((2, nch, 2, high, cw) if z["tree"] else (8, HB), F32),
            pltpu.VMEM((nch, 2, tokens, cw), F32),
            pltpu.VMEM((ties, nch, 2 * tt, cw), BF16),
            pltpu.VMEM((ties, nch, 2 * tt, cw), BF16),
            pltpu.VMEM((ndp, tt, HB), F32),
            dma(chips), dma(nt), dma(nt), dma(ndp), dma(ndp), dma(chips), dma(chips),
            dma(others, nch), dma(others, nch), dma(ties, nch), dma(ties, nch),
            dma(ndp), dma(ndp),
        ],
        compiler_params=pltpu.CompilerParams(
            collective_id=0, has_side_effects=True, vmem_limit_bytes=56 * 2 ** 20),
    )(activations, weight_codes, scale_index.T, scale_table, bit_widths[0].T,
      jnp.asarray(sylvester(HB), BF16))
    return out, scores[:, 0][None]


def solution(mesh):
    in_specs = (
        P("dp", "tensor"),
        P(("tensor", "dp"), None),
        P(("tensor", "dp"), None),
        P(),
        P(None, ("tensor", "dp"), None),
    )
    out_specs = (P("tensor", "dp"), P(None, "tensor"))
    body = functools.partial(local, mesh.shape["dp"], mesh.shape["tensor"])
    return jax.shard_map(body, mesh=mesh, in_specs=in_specs, out_specs=out_specs, check_vma=False)
```
